32 devices in a mesh: gx: 4 (over x, core), gy: 2 (over y), gz: 4 (over z).
Axes of the slice: x: 2, y: 2, z: 4, core: 2. Of those that a mesh axis runs over, the one named last changes fastest.
Arguments:
- magnet: float32 [3, 16, 128, 512], P(None, 'gz', 'gx', 'gy'), may hold values from -1 to 1, as said below
- grains: int32 [16, 128, 512], P('gz', 'gx', 'gy'), may hold values from 0 to 15
- stiffness_table: float32 [16], replicated, may hold values from 0.2 to 1
- saturation_table: float32 [16], replicated, may hold values from 0.6 to 1.4
- kernel_x: bfloat16 [8, 128], replicated, may hold values from -3 to 3
- kernel_y: bfloat16 [8, 512], replicated, may hold values from -3 to 3
- kernel_z: bfloat16 [8, 16], replicated, may hold values from -3 to 3
- mixing: float32 [8, 3, 3], replicated, may hold values from -1.25 to 1.25
Outputs:
- magnet_next: float32 [3, 16, 128, 512], P(None, 'gz', 'gx', 'gy')
- demag_field: float32 [8, 3, 64, 256], P('gz', None, 'gx', 'gy')
The draws below stay inside these ranges and needn't reach their ends.
Inputs may be any that keep to these rules, and one draw needn't show every extreme that they name: `magnet`: every cell's three components form a unit vector.
All inputs are finite; a program needn't handle non-finite values.
Results may differ from the reference program's by a relative error of at most 0.00085.
The reference program's roundings to bfloat16 on the way (of `coarse`, `along_x` and `along_y`) count: a program that leaves them out, or rounds other values in their place, can miss the bound.
Values may be sent and summed in bfloat16 or wider, within the bound.
A program may use at most 128 MiB of HBM per device.

```python
import math
import jax
import jax.numpy as jnp
from jax import lax

RANK = 8
MATS = 16
SUBSTEPS = 3
NX = 128
NY = 512
NZ = 16
GX = 64
GY = 256
GZ = 8


def draw_magnet(key, part):
    key_height, key_angle = jax.random.split(jax.random.fold_in(key, 3))
    height = jax.random.uniform(key_height, (NZ, NX, NY), jnp.float32, -1.0, 1.0)
    angle = jax.random.uniform(key_angle, (NZ, NX, NY), jnp.float32, -math.pi, math.pi)
    radial = jnp.sqrt(jnp.maximum(1.0 - height * height, 0.0))
    return jnp.stack([radial * jnp.cos(angle), radial * jnp.sin(angle), height]).astype(jnp.float32)


def kernel_line(key, extent):
    key_reach, key_values = jax.random.split(key)
    reach_len = extent * jnp.exp(jax.random.uniform(key_reach, (RANK, 1), jnp.float32, math.log(0.15), math.log(0.6)))
    offsets = jnp.arange(2 * extent, dtype=jnp.float32) - extent
    values = jnp.clip(jax.random.normal(key_values, (RANK, 2 * extent), jnp.float32), -4.0, 4.0)
    falloff = jnp.exp(-jnp.abs(offsets)[None] / reach_len) / jnp.sqrt(reach_len)
    centre = jnp.where(offsets == 0.0, 1.0, 0.0)[None]
    return (0.8 * values * falloff + centre).astype(jnp.bfloat16)


def draw_kernel_x(key, part):
    return kernel_line(jax.random.fold_in(key, 11), GX)


def draw_kernel_y(key, part):
    return kernel_line(jax.random.fold_in(key, 12), GY)


def draw_kernel_z(key, part):
    return kernel_line(jax.random.fold_in(key, 13), GZ)


def touch_ends(result, rng, smallest, high):
    dims = result.shape
    place = [jax.random.randint(jax.random.fold_in(rng, axis), (), 0, dims[axis]) for axis in range(len(dims))]
    result = result.at[tuple(place)].set(smallest)
    longest = dims.index(max(dims))
    place[longest] = (place[longest] + 1) % dims[longest]
    return result.at[tuple(place)].set(high)


def scatter_about(key, shape, deviation, reach, held_as=jnp.bfloat16):
    result = jax.random.normal(key, shape, jnp.float32) * deviation
    return jnp.minimum(jnp.maximum(result, -reach), reach).astype(held_as)


def setup_inputs(seed: int = 0) -> dict:
    key_of = jax.random.split(jax.random.key(seed), 9)
    magnet = draw_magnet(jax.random.fold_in(key_of[8], 71), 0)
    grains = touch_ends(jax.random.randint(key_of[1], (NZ, NX, NY), 0, MATS), jax.random.fold_in(key_of[1], 1), 0, MATS - 1).astype(jnp.int32)
    stiffness_table = jnp.clip(jnp.exp(jax.random.uniform(key_of[2], (MATS,), jnp.float32, math.log(0.2), math.log(1.0))), 0.2, 1.0)
    saturation_table = jnp.clip(jax.random.uniform(key_of[3], (MATS,), jnp.float32, 0.6, 1.4), 0.6, 1.4)
    kernel_x = draw_kernel_x(jax.random.fold_in(key_of[8], 71), 0)
    kernel_y = draw_kernel_y(jax.random.fold_in(key_of[8], 71), 0)
    kernel_z = draw_kernel_z(jax.random.fold_in(key_of[8], 71), 0)
    mixing = scatter_about(key_of[7], (RANK, 3, 3), (3 * RANK) ** -0.5, 1.25, jnp.float32)
    return dict(magnet=magnet, grains=grains, stiffness_table=stiffness_table, saturation_table=saturation_table, kernel_x=kernel_x, kernel_y=kernel_y, kernel_z=kernel_z, mixing=mixing)


time_step = 0.02
damping = 0.3

def toeplitz_rows(kernel, offset, extent):
    length = kernel.shape[1] // 2
    flipped = kernel[:, ::-1]
    row_ids = offset + jnp.arange(extent, dtype=jnp.int32)
    picked = jax.vmap(lambda row_index: lax.dynamic_slice_in_dim(flipped, (length - 1 - row_index).astype(jnp.int32), length, 1))(row_ids)
    return jnp.transpose(picked, (1, 0, 2))

def interior(values):
    return values[..., 1:-1, 1:-1, 1:-1]

def shifted(values, along, begin_at):
    slicer = [slice(1, -1), slice(1, -1), slice(1, -1)]
    slicer[along] = slice(begin_at, begin_at + values.shape[along - 3] - 2)
    leading = [slice(None)] * (values.ndim - 3)
    return values[tuple(leading + slicer)]

def cross_product(first_vec, second_vec):
    return jnp.stack([first_vec[1] * second_vec[2] - first_vec[2] * second_vec[1], first_vec[2] * second_vec[0] - first_vec[0] * second_vec[2], first_vec[0] * second_vec[1] - first_vec[1] * second_vec[0]])

def exchange_update(magnet_rim, stiff_rim, saturation, demag_fine):
    centre = interior(magnet_rim)
    stiff_centre = interior(stiff_rim)
    coupled = jnp.zeros_like(centre)
    for along in range(3):
        for begin_at in (0, 2):
            stiff_near = shifted(stiff_rim, along, begin_at)
            denominator = stiff_centre + stiff_near
            weight = 2.0 * stiff_centre * stiff_near / jnp.where(denominator > 0.0, denominator, 1.0)
            coupled = coupled + weight[None] * (shifted(magnet_rim, along, begin_at) - centre)
    inside = saturation > 0.0
    safe_sat = jnp.where(inside, saturation, 1.0)
    field_total = 2.0 * coupled / safe_sat[None] + demag_fine
    torque = cross_product(centre, field_total)
    raw_next = centre - time_step * (torque + damping * cross_product(centre, torque))
    length_sq = jnp.sqrt(lax.optimization_barrier(jnp.sum(raw_next * raw_next, axis=0)))
    safe_len = jnp.where(inside, length_sq, 1.0)
    return jnp.where(inside[None], raw_next / safe_len[None], 0.0)

def coarsen(magnet, saturation):
    weighted = saturation[None] * magnet
    comps, depth, width, height = weighted.shape
    shaped = weighted.reshape(comps, depth // 2, 2, width // 2, 2, height // 2, 2)
    return lax.optimization_barrier(jnp.mean(shaped, axis=(2, 4, 6))).astype(jnp.bfloat16)

def prolong(demag):
    moved = jnp.transpose(demag, (1, 0, 2, 3))
    return jnp.repeat(jnp.repeat(jnp.repeat(moved, 2, axis=1), 2, axis=2), 2, axis=3)

def reference(magnet, grains, stiffness_table, saturation_table, kernel_x, kernel_y, kernel_z, mixing):
    stiffness = stiffness_table[grains]
    saturation = saturation_table[grains]
    coarse = coarsen(magnet, saturation)
    whole_z = toeplitz_rows(kernel_z, 0, kernel_z.shape[1] // 2).astype(jnp.float32)

    def one_rank(running, inputs):
        line_x, line_y, matrix_z, mix_rank = inputs
        matrix_x = toeplitz_rows(line_x[None], 0, line_x.shape[0] // 2)[0].astype(jnp.float32)
        matrix_y = toeplitz_rows(line_y[None], 0, line_y.shape[0] // 2)[0].astype(jnp.float32)
        along_x = jnp.einsum('ab,jzby->jzay', matrix_x, coarse.astype(jnp.float32)).astype(jnp.bfloat16)
        along_y = jnp.einsum('by,jzxy->jzxb', matrix_y, along_x.astype(jnp.float32)).astype(jnp.bfloat16)
        weights = jnp.einsum('ij,az->aijz', mix_rank, matrix_z, precision=lax.Precision.HIGHEST)
        added = jnp.einsum('aijz,jzxy->aixy', weights, along_y.astype(jnp.float32), precision=lax.Precision.HIGHEST)
        return (running + added, None)
    start_field = jnp.zeros((coarse.shape[1], 3, coarse.shape[2], coarse.shape[3]), jnp.float32)
    demag, unused = lax.scan(one_rank, start_field, (kernel_x, kernel_y, whole_z, mixing))
    demag_fine = prolong(demag)
    stiff_rim = jnp.pad(stiffness, 1)
    state = magnet
    for substep in range(SUBSTEPS):
        magnet_rim = jnp.pad(state, ((0, 0), (1, 1), (1, 1), (1, 1)))
        state = exchange_update(magnet_rim, stiff_rim, saturation, demag_fine)
    return (state, demag)
```

```python
import functools

import jax
import jax.numpy as jnp
from jax import lax
from jax.experimental import pallas as pl
from jax.experimental.pallas import tpu as pltpu
from jax.sharding import PartitionSpec as P

SUBSTEPS = 3
TIME_STEP = 0.02
DAMPING = 0.3
LANES = 128
HIGHEST = lax.Precision.HIGHEST
MESH = pl.DeviceIdType.MESH
F32 = jnp.float32
BF16 = jnp.bfloat16


def kernel(
    dims,
    magnet, grains, stiff_tab, sat_tab, kx, ky, kz, mix,
    out_m, out_d,
    state, stiff, inv_sat, weights, pooled_in, pooled, gathered, kx32, ky32, kz32, flat_x,
    mat_x, mat_y, trans_x, mixed, z_send, z_recv, fine,
    xs, xr, ys, yr, zs, zr,
    g_send, g_recv, s_send, s_recv, h_send, h_recv,
):
    cx, cy, cz = dims
    comps, nz, nx, ny = magnet.shape
    rank = kx.shape[0]
    mats = stiff_tab.shape[0]
    rz, rx, ry = nz // 2, nx // 2, ny // 2
    gx_all, gy_all, gz_all = rx * cx, ry * cy, rz * cz
    jz = comps * rz
    ix, iy, iz = lax.axis_index("gx"), lax.axis_index("gy"), lax.axis_index("gz")
    plane = cx * cy
    me = ix * cy + iy

    def spot(number):
        return lax.div(number, cy), lax.rem(number, cy)

    barrier = pltpu.get_barrier_semaphore()
    for d in range(1, plane):
        tx, ty = spot(lax.rem(me + d, plane))
        pl.semaphore_signal(
            barrier, inc=1, device_id={"gx": tx, "gy": ty, "gz": iz}, device_id_type=MESH
        )
    for d in range(1, cz):
        pl.semaphore_signal(
            barrier, inc=1,
            device_id={"gx": ix, "gy": iy, "gz": lax.rem(iz + d, cz)}, device_id_type=MESH,
        )

    row = lax.broadcasted_iota(jnp.int32, (nx, ny), 0)
    lane = lax.broadcasted_iota(jnp.int32, (nx, ny), 1)
    pack_lane = lax.broadcasted_iota(jnp.int32, (nx, LANES), 1)

    for zc in range(rz):
        sums = [None] * comps
        for half in range(2):
            z = 2 * zc + half
            g = grains[z]
            a = jnp.full((nx, ny), stiff_tab[0], F32)
            s = jnp.full((nx, ny), sat_tab[0], F32)
            for k in range(1, mats):
                hit = g == k
                a = jnp.where(hit, stiff_tab[k], a)
                s = jnp.where(hit, sat_tab[k], s)
            stiff[z] = a
            inv_sat[z] = 2.0 / s
            for j in range(comps):
                m = magnet[j, z]
                state[0, j, z + 1] = m
                sums[j] = s * m if half == 0 else sums[j] + s * m
        for j in range(comps):
            pooled_in[(j * rz + zc) * nx:(j * rz + zc + 1) * nx, :] = sums[j]
    fold = (
        lax.broadcasted_iota(jnp.int32, (ny, ry), 0) // 2
        == lax.broadcasted_iota(jnp.int32, (ny, ry), 1)
    ).astype(F32)
    pooled[...] = jnp.dot(
        pooled_in[...], fold, precision=HIGHEST, preferred_element_type=F32
    )
    coarse = 0.125 * (
        pooled[pl.ds(0, jz * rx, 2), :] + pooled[pl.ds(1, jz * rx, 2), :]
    )

    def block_of(px, py):
        return gathered.at[
            :, pl.ds(pl.multiple_of(px * rx, rx), rx), pl.ds(pl.multiple_of(py * ry, ry), ry)
        ]

    block_of(ix, iy)[...] = coarse.astype(BF16).reshape(jz, rx, ry)

    def pack(step, k, value, edges):
        xs[step, 0, k:k + 1, :] = value[0:1, :]
        xs[step, 1, k:k + 1, :] = value[nx - 1:nx, :]
        hit = pack_lane == k
        return (
            jnp.where(hit, value[:, 0:1], edges[0]),
            jnp.where(hit, value[:, ny - 1:ny], edges[1]),
        )

    edges = (jnp.zeros((nx, LANES), F32),) * 2
    for j in range(comps + 1):
        for z in range(nz):
            value = magnet[j, z] if j < comps else stiff[z]
            edges = pack(0, j * nz + z, value, edges)
            if z == 0:
                zs[0, 0, j] = value.astype(BF16)
            if z == nz - 1:
                zs[0, 1, j] = value.astype(BF16)
    ys[0, 0], ys[0, 1] = edges

    pl.semaphore_wait(barrier, plane - 1 + cz - 1)

    def gather_copy(d, source):
        px, py = spot(source)
        tx, ty = spot(lax.rem(me + d, plane))
        return pltpu.make_async_remote_copy(
            src_ref=block_of(px, py), dst_ref=block_of(px, py),
            send_sem=g_send.at[d - 1], recv_sem=g_recv.at[d - 1],
            device_id={"gx": tx, "gy": ty, "gz": iz}, device_id_type=MESH,
        )

    for d in range(1, plane):
        gather_copy(d, me).start()

    places = (ix, iy, iz)
    counts = (cx, cy, cz)
    names = ("gx", "gy", "gz")

    def halo_copy(step, axis, way):
        sends, recvs = ((xs, xr), (ys, yr), (zs, zr))[axis]
        src, dst = sends.at[step, way], recvs.at[step, 1 - way]
        if axis == 2 and step > 0:
            src, dst = src.at[0:comps], dst.at[0:comps]
        target = dict(zip(names, places))
        target[names[axis]] = places[axis] + (2 * way - 1)
        return pltpu.make_async_remote_copy(
            src_ref=src, dst_ref=dst,
            send_sem=h_send.at[step, axis, way], recv_sem=h_recv.at[step, axis, way],
            device_id=target, device_id_type=MESH,
        )

    def can_send(axis, way):
        return places[axis] > 0 if way == 0 else places[axis] < counts[axis] - 1

    def send_halos(step):
        for axis in (2, 1, 0):
            for way in range(2):
                @pl.when(can_send(axis, way))
                def _():
                    halo_copy(step, axis, way).start()

    def receive_halos(step):
        for axis in range(3):
            for way in range(2):
                @pl.when(can_send(axis, 1 - way))
                def _():
                    halo_copy(step, axis, way).wait_recv()

    send_halos(0)

    for axis in range(3):
        recvs = (xr, yr, zr)[axis]
        for way in range(2):
            @pl.when(jnp.logical_not(can_send(axis, way)))
            def _():
                for step in range(SUBSTEPS):
                    recvs[step, way] = jnp.zeros(recvs.shape[2:], recvs.dtype)

    kx32[...] = kx[...].astype(F32)
    ky32[...] = ky[...].astype(F32)
    kz32[...] = jnp.zeros_like(kz32)
    kz32[:, 0:kz.shape[1]] = kz[...].astype(F32)

    def skewed(line, width):
        rows = jnp.broadcast_to(line, (8, width))
        place = lax.broadcasted_iota(jnp.int32, (8, width), 0)
        for step in (1, 2, 4):
            rows = jnp.where(place & step != 0, pltpu.roll(rows, step, 1), rows)
        return rows

    wide = 2 * gx_all
    lane_x = lax.broadcasted_iota(jnp.int32, (8, wide), 1)
    kx_here = pltpu.roll(kx32[...], lax.rem(2 * wide - gx_all - ix * rx, wide), 1)
    bases = [skewed(kx_here[r:r + 1, :], wide) for r in range(rank)]
    for t in range(gx_all // 8):
        block = jnp.zeros((8, wide), F32)
        for r in range(rank):
            turned = pltpu.roll(bases[r], (8 * t + r * rx) % wide, 1)
            block = jnp.where(lane_x // rx == r, turned, block)
        flat_x[8 * t:8 * t + 8, :] = block[:, 0:rank * rx]
    mat_x[...] = jnp.transpose(flat_x[...]).astype(BF16)
    for c in range(cy):
        start = pl.multiple_of(ry * (iy - c) + gy_all - ry, ry)
        window = ky32[:, pl.ds(start, 2 * ry)]
        for r in range(rank):
            base = skewed(window[r:r + 1, :], 2 * ry)
            for t in range(0, ry // 8, 2):
                pair = jnp.concatenate(
                    [pltpu.roll(base, 8 * (t + e) + ry, 1)[:, 0:ry] for e in range(2)], axis=0
                )
                mat_y[r, c * ry + 8 * t:c * ry + 8 * t + 16, :] = pair.astype(BF16)

    for d in range(1, plane):
        gather_copy(d, lax.rem(me + plane - d, plane)).wait_recv()

    for t in range(jz):
        along = jnp.dot(mat_x[...], gathered[t], preferred_element_type=F32).astype(BF16)
        trans_x[:, t * rx:(t + 1) * rx, :] = along.reshape(rank, rx, gy_all)
    for r in range(rank):
        along = jnp.dot(trans_x[r], mat_y[r], preferred_element_type=F32)
        along = along.astype(BF16).astype(F32).reshape(comps, rz, rx, ry)
        for i in range(comps):
            total = mix[r, i, 0] * along[0]
            for j in range(1, comps):
                total = total + mix[r, i, j] * along[j]
            mixed[r, i] = total
    turned_z = pltpu.roll(kz32[...], lax.rem(LANES + rz - 1 + rz * iz - gz_all, LANES), 1)

    def sum_copy(peer, slot):
        return pltpu.make_async_remote_copy(
            src_ref=z_send.at[peer], dst_ref=z_recv.at[slot],
            send_sem=s_send.at[peer], recv_sem=s_recv.at[slot],
            device_id={"gx": ix, "gy": iy, "gz": jnp.int32(peer)}, device_id_type=MESH,
        )

    for p in range(cz):
        totals = [[jnp.zeros((rx, ry), F32) for _ in range(comps)] for _ in range(rz)]
        for r in range(rank):
            for al in range(rz):
                for zl in range(rz):
                    at = p * rz + al - zl + rz - 1
                    factor = turned_z[r:r + 1, at:at + 1]
                    for i in range(comps):
                        totals[al][i] = totals[al][i] + factor * mixed[r, i, zl]
        for al in range(rz):
            for i in range(comps):
                z_send[p, al, i] = totals[al][i]

        @pl.when(iz != p)
        def _():
            sum_copy(p, iz).start()

        @pl.when(iz == p)
        def _():
            z_recv[p] = z_send[p]

    receive_halos(0)

    def around(value, step, k):
        return (
            jnp.where(row == 0, xr[step, 0, k:k + 1, :], pltpu.roll(value, 1, 0)),
            jnp.where(row == nx - 1, xr[step, 1, k:k + 1, :], pltpu.roll(value, nx - 1, 0)),
            jnp.where(lane == 0, yr[step, 0][:, k:k + 1], pltpu.roll(value, 1, 1)),
            jnp.where(lane == ny - 1, yr[step, 1][:, k:k + 1], pltpu.roll(value, ny - 1, 1)),
        )

    for z in range(nz):
        here = stiff[z]
        below = zr[0, 0, comps].astype(F32) if z == 0 else stiff[z - 1]
        above = zr[0, 1, comps].astype(F32) if z == nz - 1 else stiff[z + 1]
        scale = 2.0 * inv_sat[z] * here
        for n, near in enumerate(around(here, 0, comps * nz + z) + (below, above)):
            weights[n, z] = scale * near / (here + near)

    for p in range(cz):
        @pl.when(iz != p)
        def _():
            sum_copy(p, p).wait_recv()

    total = z_recv[0]
    for p in range(1, cz):
        total = total + z_recv[p]
    out_d[...] = total
    unfold = (
        lax.broadcasted_iota(jnp.int32, (ry, ny), 1) // 2
        == lax.broadcasted_iota(jnp.int32, (ry, ny), 0)
    ).astype(F32)
    spread = jnp.dot(
        total.reshape(rz * comps * rx, ry), unfold, precision=HIGHEST,
        preferred_element_type=F32,
    )
    for part in range(2):
        piece = spread[:, part * ry:(part + 1) * ry]
        for odd in range(2):
            fine.at[part][pl.ds(odd, rz * comps * rx, 2), :] = piece

    for step in range(SUBSTEPS):
        now, later = step % 2, (step + 1) % 2
        last = step == SUBSTEPS - 1
        if step > 0:
            receive_halos(step)
        for j in range(comps):
            state[now, j, 0] = zr[step, 0, j].astype(F32)
            state[now, j, nz + 1] = zr[step, 1, j].astype(F32)
        edges = (jnp.zeros((nx, LANES), F32),) * 2
        for z in range(nz):
            m, h = [], []
            for j in range(comps):
                value = state[now, j, z + 1]
                at = ((z // 2) * comps + j) * nx
                field = jnp.concatenate([fine[0, at:at + nx, :], fine[1, at:at + nx, :]], axis=1)
                near = around(value, step, j * nz + z) + (
                    state[now, j, z], state[now, j, z + 2]
                )
                for n in range(6):
                    field = field + weights[n, z] * near[n]
                m.append(value)
                h.append(field)
            t = [
                m[1] * h[2] - m[2] * h[1],
                m[2] * h[0] - m[0] * h[2],
                m[0] * h[1] - m[1] * h[0],
            ]
            u = [
                m[1] * t[2] - m[2] * t[1],
                m[2] * t[0] - m[0] * t[2],
                m[0] * t[1] - m[1] * t[0],
            ]
            raw = [m[j] - TIME_STEP * (t[j] + DAMPING * u[j]) for j in range(comps)]
            shrink = lax.rsqrt(raw[0] * raw[0] + raw[1] * raw[1] + raw[2] * raw[2])
            for j in range(comps):
                value = raw[j] * shrink
                if last:
                    out_m[j, z] = value
                    continue
                state[later, j, z + 1] = value
                edges = pack(step + 1, j * nz + z, value, edges)
                if z == 0:
                    zs[step + 1, 0, j] = value.astype(BF16)
                if z == nz - 1:
                    zs[step + 1, 1, j] = value.astype(BF16)
        if not last:
            ys[step + 1, 0], ys[step + 1, 1] = edges
            send_halos(step + 1)

    for d in range(1, plane):
        gather_copy(d, me).wait_send()
    for p in range(cz):
        @pl.when(iz != p)
        def _():
            sum_copy(p, iz).wait_send()
    for step in range(SUBSTEPS):
        for axis in range(3):
            for way in range(2):
                @pl.when(can_send(axis, way))
                def _():
                    halo_copy(step, axis, way).wait_send()


def local(dims, magnet, grains, stiff_tab, sat_tab, kx, ky, kz, mix):
    cx, cy, cz = dims
    comps, nz, nx, ny = magnet.shape
    rank = kx.shape[0]
    rz, rx, ry = nz // 2, nx // 2, ny // 2
    jz = comps * rz
    gx_all, gy_all = rx * cx, ry * cy
    packed = (comps + 1) * nz
    vmem = pl.BlockSpec(memory_space=pltpu.VMEM)
    smem = pl.BlockSpec(memory_space=pltpu.SMEM)
    dma = pltpu.SemaphoreType.DMA
    return pl.pallas_call(
        functools.partial(kernel, dims),
        out_shape=(
            jax.ShapeDtypeStruct(magnet.shape, F32),
            jax.ShapeDtypeStruct((rz, comps, rx, ry), F32),
        ),
        in_specs=[vmem, vmem, smem, smem, vmem, vmem, vmem, smem],
        out_specs=(vmem, vmem),
        scratch_shapes=[
            pltpu.VMEM((2, comps, nz + 2, nx, ny), F32),
            pltpu.VMEM((nz, nx, ny), F32),
            pltpu.VMEM((nz, nx, ny), F32),
            pltpu.VMEM((6, nz, nx, ny), F32),
            pltpu.VMEM((jz * nx, ny), F32),
            pltpu.VMEM((jz * nx, ry), F32),
            pltpu.VMEM((jz, gx_all, gy_all), BF16),
            pltpu.VMEM(kx.shape, F32),
            pltpu.VMEM(ky.shape, F32),
            pltpu.VMEM((rank, LANES), F32),
            pltpu.VMEM((gx_all, rank * rx), F32),
            pltpu.VMEM((rank * rx, gx_all), BF16),
            pltpu.VMEM((rank, gy_all, ry), BF16),
            pltpu.VMEM((rank, jz * rx, gy_all), BF16),
            pltpu.VMEM((rank, comps, rz, rx, ry), F32),
            pltpu.VMEM((cz, rz, comps, rx, ry), F32),
            pltpu.VMEM((cz, rz, comps, rx, ry), F32),
            pltpu.VMEM((2, jz * nx, ry), F32),
            pltpu.VMEM((SUBSTEPS, 2, packed, ny), F32),
            pltpu.VMEM((SUBSTEPS, 2, packed, ny), F32),
            pltpu.VMEM((SUBSTEPS, 2, nx, LANES), F32),
            pltpu.VMEM((SUBSTEPS, 2, nx, LANES), F32),
            pltpu.VMEM((SUBSTEPS, 2, comps + 1, nx, ny), BF16),
            pltpu.VMEM((SUBSTEPS, 2, comps + 1, nx, ny), BF16),
            dma((cx * cy - 1,)),
            dma((cx * cy - 1,)),
            dma((cz,)),
            dma((cz,)),
            dma((SUBSTEPS, 3, 2)),
            dma((SUBSTEPS, 3, 2)),
        ],
        compiler_params=pltpu.CompilerParams(
            collective_id=0, has_side_effects=True, vmem_limit_bytes=40 * 1024 * 1024
        ),
    )(magnet, grains, stiff_tab, sat_tab, kx, ky, kz, mix)


def solution(mesh):
    dims = tuple(mesh.shape[name] for name in ("gx", "gy", "gz"))
    in_specs = (P(None, "gz", "gx", "gy"), P("gz", "gx", "gy"), P(), P(), P(), P(), P(), P())
    out_specs = (P(None, "gz", "gx", "gy"), P("gz", None, "gx", "gy"))
    return jax.shard_map(
        functools.partial(local, dims), mesh=mesh, in_specs=in_specs, out_specs=out_specs,
        check_vma=False,
    )
```

```python
import functools

import jax
import jax.numpy as jnp
from jax import lax
from jax.experimental import pallas as pl
from jax.experimental.pallas import tpu as pltpu
from jax.sharding import PartitionSpec as P

SUBSTEPS = 3
TIME_STEP = 0.02
DAMPING = 0.3
LANES = 128
HIGHEST = lax.Precision.HIGHEST
MESH = pl.DeviceIdType.MESH
F32 = jnp.float32
BF16 = jnp.bfloat16


def kernel(
    dims,
    magnet_in, grains_in, stiff_tab, sat_tab, kx, ky, kz, mix,
    out_m, out_d,
    state, grains, stiff, inv_sat, weights, weight_x, weight_y, field_in, pooled_in, pooled, gathered, kx32, ky32, kz32, flat_x,
    mat_x, mat_y, trans_x, mixed, z_send, z_recv, fine,
    xs, xr, ys, yr, zs, zr,
    g_send, g_recv, s_send, s_recv, h_send, h_recv, in_sem,
):
    cx, cy, cz = dims
    comps, nz, nx, ny = magnet_in.shape
    rank = kx.shape[0]
    mats = stiff_tab.shape[0]
    rz, rx, ry = nz // 2, nx // 2, ny // 2
    gx_all, gy_all, gz_all = rx * cx, ry * cy, rz * cz
    jz = comps * rz
    ix, iy, iz = lax.axis_index("gx"), lax.axis_index("gy"), lax.axis_index("gz")
    plane = cx * cy
    me = ix * cy + iy

    def spot(number):
        return lax.div(number, cy), lax.rem(number, cy)

    def load(zc):
        pair = pl.ds(2 * zc, 2)
        return (
            pltpu.make_async_copy(grains_in.at[pair], grains.at[pair], in_sem.at[zc, 0]),
            pltpu.make_async_copy(
                magnet_in.at[:, pair], state.at[0, :, pair], in_sem.at[zc, 1]
            ),
        )

    for zc in range(rz):
        for copy in load(zc):
            copy.start()

    barrier = pltpu.get_barrier_semaphore()
    for d in range(1, plane):
        tx, ty = spot(lax.rem(me + d, plane))
        pl.semaphore_signal(
            barrier, inc=1, device_id={"gx": tx, "gy": ty, "gz": iz}, device_id_type=MESH
        )
    for d in range(1, cz):
        pl.semaphore_signal(
            barrier, inc=1,
            device_id={"gx": ix, "gy": iy, "gz": lax.rem(iz + d, cz)}, device_id_type=MESH,
        )

    row = lax.broadcasted_iota(jnp.int32, (nx, ny), 0)
    lane = lax.broadcasted_iota(jnp.int32, (nx, ny), 1)
    pack_lane = lax.broadcasted_iota(jnp.int32, (nx, LANES), 1)

    kx32[...] = kx[...].astype(F32)
    ky32[...] = ky[...].astype(F32)
    kz32[...] = jnp.zeros_like(kz32)
    kz32[:, 0:kz.shape[1]] = kz[...].astype(F32)

    def skewed(line, width):
        rows = jnp.broadcast_to(line, (8, width))
        place = lax.broadcasted_iota(jnp.int32, (8, width), 0)
        for step in (1, 2, 4):
            rows = jnp.where(place & step != 0, pltpu.roll(rows, step, 1), rows)
        return rows

    wide = 2 * gx_all
    lane_x = lax.broadcasted_iota(jnp.int32, (8, wide), 1)
    kx_here = pltpu.roll(kx32[...], lax.rem(2 * wide - gx_all - ix * rx, wide), 1)
    bases = [skewed(kx_here[r:r + 1, :], wide) for r in range(rank)]
    for t in range(gx_all // 8):
        block = jnp.zeros((8, wide), F32)
        for r in range(rank):
            turned = pltpu.roll(bases[r], (8 * t + r * rx) % wide, 1)
            block = jnp.where(lane_x // rx == r, turned, block)
        flat_x[8 * t:8 * t + 8, :] = block[:, 0:rank * rx]
    mat_x[...] = jnp.transpose(flat_x[...]).astype(BF16)
    def lookup(g, table):
        value = jnp.full((nx, ny), table[0], F32)
        for k in range(1, mats):
            value = jnp.where(g == k, table[k], value)
        return value

    for zc in range(rz):
        for copy in load(zc):
            copy.wait()
        sums = [None] * comps
        for half in range(2):
            z = 2 * zc + half
            s = lookup(grains[z], sat_tab)
            inv_sat[z] = 2.0 / s
            for j in range(comps):
                m = state[0, j, z]
                sums[j] = s * m if half == 0 else sums[j] + s * m
        for j in range(comps):
            pooled_in[(j * rz + zc) * nx:(j * rz + zc + 1) * nx, :] = sums[j]
    fold = (
        lax.broadcasted_iota(jnp.int32, (ny, ry), 0) // 2
        == lax.broadcasted_iota(jnp.int32, (ny, ry), 1)
    ).astype(F32)
    pooled[...] = jnp.dot(
        pooled_in[...], fold, precision=HIGHEST, preferred_element_type=F32
    )
    coarse = 0.125 * (
        pooled[pl.ds(0, jz * rx, 2), :] + pooled[pl.ds(1, jz * rx, 2), :]
    )

    def block_of(px, py):
        return gathered.at[
            :, pl.ds(pl.multiple_of(px * rx, rx), rx), pl.ds(pl.multiple_of(py * ry, ry), ry)
        ]

    block_of(ix, iy)[...] = coarse.astype(BF16).reshape(jz, rx, ry)

    pl.semaphore_wait(barrier, plane - 1 + cz - 1)

    def gather_copy(d, source):
        px, py = spot(source)
        tx, ty = spot(lax.rem(me + d, plane))
        return pltpu.make_async_remote_copy(
            src_ref=block_of(px, py), dst_ref=block_of(px, py),
            send_sem=g_send.at[d - 1], recv_sem=g_recv.at[d - 1],
            device_id={"gx": tx, "gy": ty, "gz": iz}, device_id_type=MESH,
        )

    for d in range(1, plane):
        gather_copy(d, me).start()

    def pack(step, k, value, edges):
        xs[step, 0, k:k + 1, :] = value[0:1, :]
        xs[step, 1, k:k + 1, :] = value[nx - 1:nx, :]
        hit = pack_lane == k
        return (
            jnp.where(hit, value[:, 0:1], edges[0]),
            jnp.where(hit, value[:, ny - 1:ny], edges[1]),
        )

    for z in range(nz):
        stiff[z] = lookup(grains[z], stiff_tab)
    edges = (jnp.zeros((nx, LANES), F32),) * 2
    for j in range(comps + 1):
        for z in range(nz):
            value = state[0, j, z] if j < comps else stiff[z]
            edges = pack(0, j * nz + z, value, edges)
            if z == 0:
                zs[0, 0, j] = value.astype(BF16)
            if z == nz - 1:
                zs[0, 1, j] = value.astype(BF16)
    ys[0, 0], ys[0, 1] = edges

    places = (ix, iy, iz)
    counts = (cx, cy, cz)
    names = ("gx", "gy", "gz")

    def halo_copy(step, axis, way):
        sends, recvs = ((xs, xr), (ys, yr), (zs, zr))[axis]
        src, dst = sends.at[step, way], recvs.at[step, 1 - way]
        if axis == 2 and step > 0:
            src, dst = src.at[0:comps], dst.at[0:comps]
        target = dict(zip(names, places))
        target[names[axis]] = places[axis] + (2 * way - 1)
        return pltpu.make_async_remote_copy(
            src_ref=src, dst_ref=dst,
            send_sem=h_send.at[step, axis, way], recv_sem=h_recv.at[step, axis, way],
            device_id=target, device_id_type=MESH,
        )

    def can_send(axis, way):
        return places[axis] > 0 if way == 0 else places[axis] < counts[axis] - 1

    def send_halos(step, axes):
        for axis in axes:
            for way in range(2):
                @pl.when(can_send(axis, way))
                def _():
                    halo_copy(step, axis, way).start()

    def receive_halos(step):
        for axis in range(3):
            for way in range(2):
                @pl.when(can_send(axis, 1 - way))
                def _():
                    halo_copy(step, axis, way).wait_recv()

    send_halos(0, (2, 1, 0))

    for axis in range(3):
        recvs = (xr, yr, zr)[axis]
        for way in range(2):
            @pl.when(jnp.logical_not(can_send(axis, way)))
            def _():
                for step in range(SUBSTEPS):
                    recvs[step, way] = jnp.zeros(recvs.shape[2:], recvs.dtype)

    for c in range(cy):
        start = pl.multiple_of(ry * (iy - c) + gy_all - ry, ry)
        window = ky32[:, pl.ds(start, 2 * ry)]
        for r in range(rank):
            base = skewed(window[r:r + 1, :], 2 * ry)
            for t in range(0, ry // 8, 2):
                pair = jnp.concatenate(
                    [pltpu.roll(base, 8 * (t + e) + ry, 1)[:, 0:ry] for e in range(2)], axis=0
                )
                mat_y[r, c * ry + 8 * t:c * ry + 8 * t + 16, :] = pair.astype(BF16)

    for d in range(1, plane):
        gather_copy(d, lax.rem(me + plane - d, plane)).wait_recv()

    for t in range(jz):
        along = jnp.dot(mat_x[...], gathered[t], preferred_element_type=F32).astype(BF16)
        trans_x[:, t * rx:(t + 1) * rx, :] = along.reshape(rank, rx, gy_all)
    for r in range(rank):
        along = jnp.dot(trans_x[r], mat_y[r], preferred_element_type=F32)
        along = along.astype(BF16).astype(F32).reshape(comps, rz, rx, ry)
        for i in range(comps):
            total = mix[i, 0, r] * along[0]
            for j in range(1, comps):
                total = total + mix[i, j, r] * along[j]
            mixed[r, i] = total
    def sum_copy(peer, slot):
        return pltpu.make_async_remote_copy(
            src_ref=z_send.at[peer], dst_ref=z_recv.at[slot],
            send_sem=s_send.at[peer], recv_sem=s_recv.at[slot],
            device_id={"gx": ix, "gy": iy, "gz": peer}, device_id_type=MESH,
        )

    for n in range(cz):
        d = (cz // 2 + n) % cz if n < cz - cz // 2 else cz - n - 1
        p = lax.rem(iz + d, cz) if d else iz
        turn = lax.rem(2 * LANES + rz - 1 + rz * (iz - p) - gz_all, LANES)
        turned_z = pltpu.roll(kz32[...], turn, 1)
        totals = [[jnp.zeros((rx, ry), F32) for _ in range(comps)] for _ in range(rz)]
        for r in range(rank):
            for al in range(rz):
                for zl in range(rz):
                    at = al - zl + rz - 1
                    factor = turned_z[r:r + 1, at:at + 1]
                    for i in range(comps):
                        totals[al][i] = totals[al][i] + factor * mixed[r, i, zl]
        target = z_send if d else z_recv
        for al in range(rz):
            for i in range(comps):
                target[p, al, i] = totals[al][i]
        if d:
            sum_copy(p, iz).start()

    receive_halos(0)

    def rolled(value):
        return (
            pltpu.roll(value, 1, 0), pltpu.roll(value, nx - 1, 0),
            pltpu.roll(value, 1, 1), pltpu.roll(value, ny - 1, 1),
        )

    row_top = lax.broadcasted_iota(jnp.int32, (8, ny), 0)
    for z in range(nz):
        here = stiff[z]
        k = comps * nz + z
        below = zr[0, 0, comps].astype(F32) if z == 0 else stiff[z - 1]
        above = zr[0, 1, comps].astype(F32) if z == nz - 1 else stiff[z + 1]
        scale = 2.0 * inv_sat[z] * here
        outside = (row == 0, row == nx - 1, lane == 0, lane == ny - 1)
        for n, near in enumerate(rolled(here)):
            weights[n, z] = jnp.where(outside[n], 0.0, scale * near / (here + near))
        weights[4, z] = scale * below / (here + below)
        weights[5, z] = scale * above / (here + above)
        for way in range(2):
            cut = slice(0, 8) if way == 0 else slice(nx - 8, nx)
            near = xr[0, way, k:k + 1, :]
            weight_x[way, z] = jnp.where(
                row_top == 7 * way, scale[cut] * near / (here[cut] + near), 0.0
            )
            cut = slice(0, LANES) if way == 0 else slice(ny - LANES, ny)
            near = yr[0, way][:, k:k + 1]
            weight_y[way, z] = jnp.where(
                pack_lane == (LANES - 1) * way,
                scale[:, cut] * near / (here[:, cut] + near), 0.0,
            )

    def inner_field(now, z, j):
        near = rolled(state[now, j, z])
        field = weights[0, z] * near[0]
        for n in range(1, 4):
            field = field + weights[n, z] * near[n]
        if z > 0:
            field = field + weights[4, z] * state[now, j, z - 1]
        if z < nz - 1:
            field = field + weights[5, z] * state[now, j, z + 1]
        return field

    def outer_field(field, step, z, j):
        k = j * nz + z
        if z == 0:
            field = field + weights[4, z] * zr[step, 0, j].astype(F32)
        if z == nz - 1:
            field = field + weights[5, z] * zr[step, 1, j].astype(F32)
        top = field[0:8] + weight_x[0, z] * xr[step, 0, k:k + 1, :]
        bottom = field[nx - 8:nx] + weight_x[1, z] * xr[step, 1, k:k + 1, :]
        field = jnp.concatenate([top, field[8:nx - 8], bottom], axis=0)
        left = field[:, 0:LANES] + weight_y[0, z] * yr[step, 0][:, k:k + 1]
        right = field[:, ny - LANES:ny] + weight_y[1, z] * yr[step, 1][:, k:k + 1]
        middle = [field[:, LANES:ny - LANES]] if ny > 2 * LANES else []
        return jnp.concatenate([left] + middle + [right], axis=1)

    for z in range(nz):
        for j in range(comps):
            field_in[j, z] = outer_field(inner_field(0, z, j), 0, z, j)

    for p in range(cz):
        @pl.when(iz != p)
        def _():
            sum_copy(jnp.int32(p), p).wait_recv()

    total = z_recv[0]
    for p in range(1, cz):
        total = total + z_recv[p]
    out_d[...] = total
    unfold = (
        lax.broadcasted_iota(jnp.int32, (ry, ny), 1) // 2
        == lax.broadcasted_iota(jnp.int32, (ry, ny), 0)
    ).astype(F32)
    spread = jnp.dot(
        total.reshape(rz * comps * rx, ry), unfold, precision=HIGHEST,
        preferred_element_type=F32,
    )
    for part in range(2):
        piece = spread[:, part * ry:(part + 1) * ry]
        for odd in range(2):
            fine.at[part][pl.ds(odd, rz * comps * rx, 2), :] = piece

    def demag_at(z, j):
        at = ((z // 2) * comps + j) * nx
        return jnp.concatenate([fine[0, at:at + nx, :], fine[1, at:at + nx, :]], axis=1)

    for step in range(SUBSTEPS):
        now, later = step % 2, (step + 1) % 2
        last = step == SUBSTEPS - 1
        if step > 0:
            receive_halos(step)
        edges = (jnp.zeros((nx, LANES), F32),) * 2
        for z in [0, nz - 1] + list(range(1, nz - 1)):
            m, h = [], []
            for j in range(comps):
                m.append(state[now, j, z])
                field = field_in[j, z]
                if step == 0:
                    h.append(field + demag_at(z, j))
                else:
                    h.append(outer_field(field, step, z, j))
            t = [
                m[1] * h[2] - m[2] * h[1],
                m[2] * h[0] - m[0] * h[2],
                m[0] * h[1] - m[1] * h[0],
            ]
            u = [
                m[1] * t[2] - m[2] * t[1],
                m[2] * t[0] - m[0] * t[2],
                m[0] * t[1] - m[1] * t[0],
            ]
            raw = [m[j] - TIME_STEP * (t[j] + DAMPING * u[j]) for j in range(comps)]
            shrink = lax.rsqrt(raw[0] * raw[0] + raw[1] * raw[1] + raw[2] * raw[2])
            for j in range(comps):
                value = raw[j] * shrink
                if last:
                    out_m[j, z] = value
                    continue
                state[later, j, z] = value
                edges = pack(step + 1, j * nz + z, value, edges)
                if z == 0:
                    zs[step + 1, 0, j] = value.astype(BF16)
                if z == nz - 1:
                    zs[step + 1, 1, j] = value.astype(BF16)
            if z == nz - 1 and not last:
                send_halos(step + 1, (2,))
        if not last:
            ys[step + 1, 0], ys[step + 1, 1] = edges
            send_halos(step + 1, (1, 0))
            for z in range(nz):
                for j in range(comps):
                    field_in[j, z] = inner_field(later, z, j) + demag_at(z, j)

    for d in range(1, plane):
        gather_copy(d, me).wait_send()
    for p in range(cz):
        @pl.when(iz != p)
        def _():
            sum_copy(jnp.int32(p), iz).wait_send()
    for step in range(SUBSTEPS):
        for axis in range(3):
            for way in range(2):
                @pl.when(can_send(axis, way))
                def _():
                    halo_copy(step, axis, way).wait_send()


def local(dims, magnet, grains, stiff_tab, sat_tab, kx, ky, kz, mix):
    cx, cy, cz = dims
    comps, nz, nx, ny = magnet.shape
    rank = kx.shape[0]
    rz, rx, ry = nz // 2, nx // 2, ny // 2
    jz = comps * rz
    gx_all, gy_all = rx * cx, ry * cy
    packed = (comps + 1) * nz
    vmem = pl.BlockSpec(memory_space=pltpu.VMEM)
    hbm = pl.BlockSpec(memory_space=pltpu.HBM)
    smem = pl.BlockSpec(memory_space=pltpu.SMEM)
    dma = pltpu.SemaphoreType.DMA
    return pl.pallas_call(
        functools.partial(kernel, dims),
        out_shape=(
            jax.ShapeDtypeStruct(magnet.shape, F32),
            jax.ShapeDtypeStruct((rz, comps, rx, ry), F32),
        ),
        in_specs=[hbm, hbm, smem, smem, vmem, vmem, vmem, smem],
        out_specs=(vmem, vmem),
        scratch_shapes=[
            pltpu.VMEM((2, comps, nz, nx, ny), F32),
            pltpu.VMEM((nz, nx, ny), jnp.int32),
            pltpu.VMEM((nz, nx, ny), F32),
            pltpu.VMEM((nz, nx, ny), F32),
            pltpu.VMEM((6, nz, nx, ny), F32),
            pltpu.VMEM((2, nz, 8, ny), F32),
            pltpu.VMEM((2, nz, nx, LANES), F32),
            pltpu.VMEM((comps, nz, nx, ny), F32),
            pltpu.VMEM((jz * nx, ny), F32),
            pltpu.VMEM((jz * nx, ry), F32),
            pltpu.VMEM((jz, gx_all, gy_all), BF16),
            pltpu.VMEM(kx.shape, F32),
            pltpu.VMEM(ky.shape, F32),
            pltpu.VMEM((rank, LANES), F32),
            pltpu.VMEM((gx_all, rank * rx), F32),
            pltpu.VMEM((rank * rx, gx_all), BF16),
            pltpu.VMEM((rank, gy_all, ry), BF16),
            pltpu.VMEM((rank, jz * rx, gy_all), BF16),
            pltpu.VMEM((rank, comps, rz, rx, ry), F32),
            pltpu.VMEM((cz, rz, comps, rx, ry), F32),
            pltpu.VMEM((cz, rz, comps, rx, ry), F32),
            pltpu.VMEM((2, jz * nx, ry), F32),
            pltpu.VMEM((SUBSTEPS, 2, packed, ny), F32),
            pltpu.VMEM((SUBSTEPS, 2, packed, ny), F32),
            pltpu.VMEM((SUBSTEPS, 2, nx, LANES), F32),
            pltpu.VMEM((SUBSTEPS, 2, nx, LANES), F32),
            pltpu.VMEM((SUBSTEPS, 2, comps + 1, nx, ny), BF16),
            pltpu.VMEM((SUBSTEPS, 2, comps + 1, nx, ny), BF16),
            dma((cx * cy - 1,)),
            dma((cx * cy - 1,)),
            dma((cz,)),
            dma((cz,)),
            dma((SUBSTEPS, 3, 2)),
            dma((SUBSTEPS, 3, 2)),
            dma((rz, 2)),
        ],
        compiler_params=pltpu.CompilerParams(
            collective_id=0, has_side_effects=True, vmem_limit_bytes=56 * 1024 * 1024
        ),
    )(magnet, grains, stiff_tab, sat_tab, kx, ky, kz, jnp.transpose(mix, (1, 2, 0)))


def solution(mesh):
    dims = tuple(mesh.shape[name] for name in ("gx", "gy", "gz"))
    in_specs = (P(None, "gz", "gx", "gy"), P("gz", "gx", "gy"), P(), P(), P(), P(), P(), P())
    out_specs = (P(None, "gz", "gx", "gy"), P("gz", None, "gx", "gy"))
    return jax.shard_map(
        functools.partial(local, dims), mesh=mesh, in_specs=in_specs, out_specs=out_specs,
        check_vma=False,
    )
```

```python
import functools

import jax
import jax.numpy as jnp
from jax import lax
from jax.experimental import pallas as pl
from jax.experimental.pallas import tpu as pltpu
from jax.sharding import PartitionSpec as P

SUBSTEPS = 3
TIME_STEP = 0.02
DAMPING = 0.3
LANES = 128
HIGHEST = lax.Precision.HIGHEST
MESH = pl.DeviceIdType.MESH
F32 = jnp.float32
BF16 = jnp.bfloat16


def kernel(
    dims,
    magnet_in, grains_in, stiff_tab, sat_tab, kx, ky, kz, mix,
    out_m, out_d,
    state, grains, stiff, inv_sat, weights, weight_x, weight_y, field_in, pooled_in, pooled, gathered, kx32, ky32, kz32, flat_x,
    mat_x, mat_y, trans_x, mixed, z_send, z_recv, fine,
    xs, xr, ys, yr, zs, zr,
    g_send, g_recv, s_send, s_recv, h_send, h_recv, in_sem,
):
    cx, cy, cz = dims
    comps, nz, nx, ny = magnet_in.shape
    rank = kx.shape[0]
    mats = stiff_tab.shape[0]
    rz, rx, ry = nz // 2, nx // 2, ny // 2
    gx_all, gy_all, gz_all = rx * cx, ry * cy, rz * cz
    jz = comps * rz
    ix, iy, iz = lax.axis_index("gx"), lax.axis_index("gy"), lax.axis_index("gz")
    plane = cx * cy
    me = ix * cy + iy

    def spot(number):
        return lax.div(number, cy), lax.rem(number, cy)

    def load(zc):
        pair = pl.ds(2 * zc, 2)
        return (
            pltpu.make_async_copy(grains_in.at[pair], grains.at[pair], in_sem.at[zc, 0]),
            pltpu.make_async_copy(
                magnet_in.at[:, pair], state.at[0, :, pair], in_sem.at[zc, 1]
            ),
        )

    for zc in range(rz):
        for copy in load(zc):
            copy.start()

    barrier = pltpu.get_barrier_semaphore()
    for d in range(1, plane):
        tx, ty = spot(lax.rem(me + d, plane))
        pl.semaphore_signal(
            barrier, inc=1, device_id={"gx": tx, "gy": ty, "gz": iz}, device_id_type=MESH
        )
    for d in range(1, cz):
        pl.semaphore_signal(
            barrier, inc=1,
            device_id={"gx": ix, "gy": iy, "gz": lax.rem(iz + d, cz)}, device_id_type=MESH,
        )

    row = lax.broadcasted_iota(jnp.int32, (nx, ny), 0)
    lane = lax.broadcasted_iota(jnp.int32, (nx, ny), 1)
    pack_lane = lax.broadcasted_iota(jnp.int32, (nx, LANES), 1)

    kx32[...] = kx[...].astype(F32)
    ky32[...] = ky[...].astype(F32)
    kz32[...] = jnp.zeros_like(kz32)
    kz32[:, 0:kz.shape[1]] = kz[...].astype(F32)

    def skewed(line, width):
        rows = jnp.broadcast_to(line, (8, width))
        place = lax.broadcasted_iota(jnp.int32, (8, width), 0)
        for step in (1, 2, 4):
            rows = jnp.where(place & step != 0, pltpu.roll(rows, step, 1), rows)
        return rows

    wide = 2 * gx_all
    lane_x = lax.broadcasted_iota(jnp.int32, (8, wide), 1)
    kx_here = pltpu.roll(kx32[...], lax.rem(2 * wide - gx_all - ix * rx, wide), 1)
    bases = [skewed(kx_here[r:r + 1, :], wide) for r in range(rank)]
    for t in range(gx_all // 8):
        block = jnp.zeros((8, wide), F32)
        for r in range(rank):
            turned = pltpu.roll(bases[r], (8 * t + r * rx) % wide, 1)
            block = jnp.where(lane_x // rx == r, turned, block)
        flat_x[8 * t:8 * t + 8, :] = block[:, 0:rank * rx]
    mat_x[...] = jnp.transpose(flat_x[...]).astype(BF16)
    def lookup(g, table):
        value = jnp.full((nx, ny), table[0], F32)
        for k in range(1, mats):
            value = jnp.where(g == k, table[k], value)
        return value

    for zc in range(rz):
        for copy in load(zc):
            copy.wait()
        sums = [None] * comps
        for half in range(2):
            z = 2 * zc + half
            s = lookup(grains[z], sat_tab)
            inv_sat[z] = 2.0 / s
            for j in range(comps):
                m = state[0, j, z]
                sums[j] = s * m if half == 0 else sums[j] + s * m
        for j in range(comps):
            pooled_in[(j * rz + zc) * nx:(j * rz + zc + 1) * nx, :] = sums[j]
    fold = (
        lax.broadcasted_iota(jnp.int32, (ny, ry), 0) // 2
        == lax.broadcasted_iota(jnp.int32, (ny, ry), 1)
    ).astype(F32)
    pooled[...] = jnp.dot(
        pooled_in[...], fold, precision=HIGHEST, preferred_element_type=F32
    )
    coarse = 0.125 * (
        pooled[pl.ds(0, jz * rx, 2), :] + pooled[pl.ds(1, jz * rx, 2), :]
    )

    def block_of(px, py):
        return gathered.at[
            :, pl.ds(pl.multiple_of(px * rx, rx), rx), pl.ds(pl.multiple_of(py * ry, ry), ry)
        ]

    block_of(ix, iy)[...] = coarse.astype(BF16).reshape(jz, rx, ry)

    pl.semaphore_wait(barrier, plane - 1 + cz - 1)

    def gather_copy(d, source):
        px, py = spot(source)
        tx, ty = spot(lax.rem(me + d, plane))
        return pltpu.make_async_remote_copy(
            src_ref=block_of(px, py), dst_ref=block_of(px, py),
            send_sem=g_send.at[d - 1], recv_sem=g_recv.at[d - 1],
            device_id={"gx": tx, "gy": ty, "gz": iz}, device_id_type=MESH,
        )

    for d in range(1, plane):
        gather_copy(d, me).start()

    def pack(step, k, value, edges):
        xs[step, 0, k:k + 1, :] = value[0:1, :]
        xs[step, 1, k:k + 1, :] = value[nx - 1:nx, :]
        hit = pack_lane == k
        return (
            jnp.where(hit, value[:, 0:1], edges[0]),
            jnp.where(hit, value[:, ny - 1:ny], edges[1]),
        )

    for z in range(nz):
        stiff[z] = lookup(grains[z], stiff_tab)
    edges = (jnp.zeros((nx, LANES), F32),) * 2
    for j in range(comps + 1):
        for z in range(nz):
            value = state[0, j, z] if j < comps else stiff[z]
            edges = pack(0, j * nz + z, value, edges)
            if z == 0:
                zs[0, 0, j] = value.astype(BF16)
            if z == nz - 1:
                zs[0, 1, j] = value.astype(BF16)
    ys[0, 0], ys[0, 1] = edges

    places = (ix, iy, iz)
    counts = (cx, cy, cz)
    names = ("gx", "gy", "gz")

    def halo_copy(step, axis, way):
        sends, recvs = ((xs, xr), (ys, yr), (zs, zr))[axis]
        src, dst = sends.at[step, way], recvs.at[step, 1 - way]
        if axis == 2 and step > 0:
            src, dst = src.at[0:comps], dst.at[0:comps]
        target = dict(zip(names, places))
        target[names[axis]] = places[axis] + (2 * way - 1)
        return pltpu.make_async_remote_copy(
            src_ref=src, dst_ref=dst,
            send_sem=h_send.at[step, axis, way], recv_sem=h_recv.at[step, axis, way],
            device_id=target, device_id_type=MESH,
        )

    def can_send(axis, way):
        return places[axis] > 0 if way == 0 else places[axis] < counts[axis] - 1

    def send_halos(step, axes):
        for axis in axes:
            for way in range(2):
                @pl.when(can_send(axis, way))
                def _():
                    halo_copy(step, axis, way).start()

    def receive_halos(step):
        for axis in range(3):
            for way in range(2):
                @pl.when(can_send(axis, 1 - way))
                def _():
                    halo_copy(step, axis, way).wait_recv()

    send_halos(0, (2, 1, 0))

    for axis in range(3):
        recvs = (xr, yr, zr)[axis]
        for way in range(2):
            @pl.when(jnp.logical_not(can_send(axis, way)))
            def _():
                for step in range(SUBSTEPS):
                    recvs[step, way] = jnp.zeros(recvs.shape[2:], recvs.dtype)

    for c in range(cy):
        start = pl.multiple_of(ry * (iy - c) + gy_all - ry, ry)
        window = ky32[:, pl.ds(start, 2 * ry)]
        for r in range(rank):
            base = skewed(window[r:r + 1, :], 2 * ry)
            for t in range(0, ry // 8, 2):
                pair = jnp.concatenate(
                    [pltpu.roll(base, 8 * (t + e) + ry, 1)[:, 0:ry] for e in range(2)], axis=0
                )
                mat_y[r, c * ry + 8 * t:c * ry + 8 * t + 16, :] = pair.astype(BF16)

    for d in range(1, plane):
        gather_copy(d, lax.rem(me + plane - d, plane)).wait_recv()

    for t in range(jz):
        along = jnp.dot(mat_x[...], gathered[t], preferred_element_type=F32).astype(BF16)
        trans_x[:, t * rx:(t + 1) * rx, :] = along.reshape(rank, rx, gy_all)
    for r in range(rank):
        along = jnp.dot(trans_x[r], mat_y[r], preferred_element_type=F32)
        along = along.astype(BF16).astype(F32).reshape(comps, rz, rx, ry)
        for i in range(comps):
            total = mix[i, 0, r] * along[0]
            for j in range(1, comps):
                total = total + mix[i, j, r] * along[j]
            mixed[r, i] = total
    def sum_copy(peer, slot):
        return pltpu.make_async_remote_copy(
            src_ref=z_send.at[peer], dst_ref=z_recv.at[slot],
            send_sem=s_send.at[peer], recv_sem=s_recv.at[slot],
            device_id={"gx": ix, "gy": iy, "gz": peer}, device_id_type=MESH,
        )

    for n in range(cz):
        d = (cz // 2 + n) % cz if n < cz - cz // 2 else cz - n - 1
        p = lax.rem(iz + d, cz) if d else iz
        turn = lax.rem(2 * LANES + rz - 1 + rz * (iz - p) - gz_all, LANES)
        turned_z = pltpu.roll(kz32[...], turn, 1)
        totals = [[jnp.zeros((rx, ry), F32) for _ in range(comps)] for _ in range(rz)]
        for r in range(rank):
            for al in range(rz):
                for zl in range(rz):
                    at = al - zl + rz - 1
                    factor = turned_z[r:r + 1, at:at + 1]
                    for i in range(comps):
                        totals[al][i] = totals[al][i] + factor * mixed[r, i, zl]
        target = z_send if d else z_recv
        for al in range(rz):
            for i in range(comps):
                target[p, al, i] = totals[al][i]
        if d:
            sum_copy(p, iz).start()

    receive_halos(0)

    def rolled(value):
        return (
            pltpu.roll(value, 1, 0), pltpu.roll(value, nx - 1, 0),
            pltpu.roll(value, 1, 1), pltpu.roll(value, ny - 1, 1),
        )

    row_top = lax.broadcasted_iota(jnp.int32, (8, ny), 0)
    for z in range(nz):
        here = stiff[z]
        k = comps * nz + z
        below = zr[0, 0, comps].astype(F32) if z == 0 else stiff[z - 1]
        above = zr[0, 1, comps].astype(F32) if z == nz - 1 else stiff[z + 1]
        scale = 2.0 * inv_sat[z] * here
        outside = (row == 0, row == nx - 1, lane == 0, lane == ny - 1)
        for n, near in enumerate(rolled(here)):
            weights[n, z] = jnp.where(outside[n], 0.0, scale * near / (here + near))
        weights[4, z] = scale * below / (here + below)
        weights[5, z] = scale * above / (here + above)
        for way in range(2):
            cut = slice(0, 8) if way == 0 else slice(nx - 8, nx)
            near = xr[0, way, k:k + 1, :]
            weight_x[way, z] = jnp.where(
                row_top == 7 * way, scale[cut] * near / (here[cut] + near), 0.0
            )
            cut = slice(0, LANES) if way == 0 else slice(ny - LANES, ny)
            near = yr[0, way][:, k:k + 1]
            weight_y[way, z] = jnp.where(
                pack_lane == (LANES - 1) * way,
                scale[:, cut] * near / (here[:, cut] + near), 0.0,
            )

    def inner_field(now, z, j):
        near = rolled(state[now, j, z])
        field = weights[0, z] * near[0]
        for n in range(1, 4):
            field = field + weights[n, z] * near[n]
        if z > 0:
            field = field + weights[4, z] * state[now, j, z - 1]
        if z < nz - 1:
            field = field + weights[5, z] * state[now, j, z + 1]
        return field

    def outer_field(field, step, z, j):
        k = j * nz + z
        if z == 0:
            field = field + weights[4, z] * zr[step, 0, j].astype(F32)
        if z == nz - 1:
            field = field + weights[5, z] * zr[step, 1, j].astype(F32)
        top = field[0:8] + weight_x[0, z] * xr[step, 0, k:k + 1, :]
        bottom = field[nx - 8:nx] + weight_x[1, z] * xr[step, 1, k:k + 1, :]
        field = jnp.concatenate([top, field[8:nx - 8], bottom], axis=0)
        left = field[:, 0:LANES] + weight_y[0, z] * yr[step, 0][:, k:k + 1]
        right = field[:, ny - LANES:ny] + weight_y[1, z] * yr[step, 1][:, k:k + 1]
        middle = [field[:, LANES:ny - LANES]] if ny > 2 * LANES else []
        return jnp.concatenate([left] + middle + [right], axis=1)

    for z in range(nz):
        for j in range(comps):
            field_in[j, z] = outer_field(inner_field(0, z, j), 0, z, j)

    for p in range(cz):
        @pl.when(iz != p)
        def _():
            sum_copy(jnp.int32(p), p).wait_recv()

    total = z_recv[0]
    for p in range(1, cz):
        total = total + z_recv[p]
    out_d[...] = total
    unfold = (
        lax.broadcasted_iota(jnp.int32, (ry, ny), 1) // 2
        == lax.broadcasted_iota(jnp.int32, (ry, ny), 0)
    ).astype(F32)
    spread = jnp.dot(
        total.reshape(rz * comps * rx, ry), unfold, precision=HIGHEST,
        preferred_element_type=F32,
    )
    for part in range(2):
        piece = spread[:, part * ry:(part + 1) * ry]
        for odd in range(2):
            fine.at[part][pl.ds(odd, rz * comps * rx, 2), :] = piece

    def demag_at(z, j):
        at = ((z // 2) * comps + j) * nx
        return jnp.concatenate([fine[0, at:at + nx, :], fine[1, at:at + nx, :]], axis=1)

    for step in range(SUBSTEPS):
        now, later = step % 2, (step + 1) % 2
        last = step == SUBSTEPS - 1
        if step > 0:
            receive_halos(step)
        edges = (jnp.zeros((nx, LANES), F32),) * 2
        for z in [0, nz - 1] + list(range(1, nz - 1)):
            m, h = [], []
            for j in range(comps):
                m.append(state[now, j, z])
                field = field_in[j, z]
                if step == 0:
                    h.append(field + demag_at(z, j))
                else:
                    h.append(outer_field(field, step, z, j))
            t = [
                m[1] * h[2] - m[2] * h[1],
                m[2] * h[0] - m[0] * h[2],
                m[0] * h[1] - m[1] * h[0],
            ]
            u = [
                m[1] * t[2] - m[2] * t[1],
                m[2] * t[0] - m[0] * t[2],
                m[0] * t[1] - m[1] * t[0],
            ]
            raw = [m[j] - TIME_STEP * (t[j] + DAMPING * u[j]) for j in range(comps)]
            shrink = lax.rsqrt(raw[0] * raw[0] + raw[1] * raw[1] + raw[2] * raw[2])
            for j in range(comps):
                value = raw[j] * shrink
                if last:
                    out_m[j, z] = value
                    continue
                state[later, j, z] = value
                edges = pack(step + 1, j * nz + z, value, edges)
                if z == 0:
                    zs[step + 1, 0, j] = value.astype(BF16)
                if z == nz - 1:
                    zs[step + 1, 1, j] = value.astype(BF16)
            if z == nz - 1 and not last:
                send_halos(step + 1, (2,))
        if not last:
            ys[step + 1, 0], ys[step + 1, 1] = edges
            send_halos(step + 1, (1, 0))
            for z in range(nz):
                for j in range(comps):
                    field_in[j, z] = inner_field(later, z, j) + demag_at(z, j)

    for d in range(1, plane):
        gather_copy(d, me).wait_send()
    for p in range(cz):
        @pl.when(iz != p)
        def _():
            sum_copy(jnp.int32(p), iz).wait_send()
    for step in range(SUBSTEPS):
        for axis in range(3):
            for way in range(2):
                @pl.when(can_send(axis, way))
                def _():
                    halo_copy(step, axis, way).wait_send()


def local(dims, magnet, grains, stiff_tab, sat_tab, kx, ky, kz, mix):
    cx, cy, cz = dims
    comps, nz, nx, ny = magnet.shape
    rank = kx.shape[0]
    rz, rx, ry = nz // 2, nx // 2, ny // 2
    jz = comps * rz
    gx_all, gy_all = rx * cx, ry * cy
    packed = (comps + 1) * nz
    vmem = pl.BlockSpec(memory_space=pltpu.VMEM)
    hbm = pl.BlockSpec(memory_space=pltpu.HBM)
    smem = pl.BlockSpec(memory_space=pltpu.SMEM)
    dma = pltpu.SemaphoreType.DMA
    return pl.pallas_call(
        functools.partial(kernel, dims),
        out_shape=(
            pltpu.VMEM(magnet.shape, F32),
            pltpu.VMEM((rz, comps, rx, ry), F32),
        ),
        in_specs=[hbm, hbm, smem, smem, vmem, vmem, vmem, smem],
        out_specs=(vmem, vmem),
        scratch_shapes=[
            pltpu.VMEM((2, comps, nz, nx, ny), F32),
            pltpu.VMEM((nz, nx, ny), jnp.int32),
            pltpu.VMEM((nz, nx, ny), F32),
            pltpu.VMEM((nz, nx, ny), F32),
            pltpu.VMEM((6, nz, nx, ny), F32),
            pltpu.VMEM((2, nz, 8, ny), F32),
            pltpu.VMEM((2, nz, nx, LANES), F32),
            pltpu.VMEM((comps, nz, nx, ny), F32),
            pltpu.VMEM((jz * nx, ny), F32),
            pltpu.VMEM((jz * nx, ry), F32),
            pltpu.VMEM((jz, gx_all, gy_all), BF16),
            pltpu.VMEM(kx.shape, F32),
            pltpu.VMEM(ky.shape, F32),
            pltpu.VMEM((rank, LANES), F32),
            pltpu.VMEM((gx_all, rank * rx), F32),
            pltpu.VMEM((rank * rx, gx_all), BF16),
            pltpu.VMEM((rank, gy_all, ry), BF16),
            pltpu.VMEM((rank, jz * rx, gy_all), BF16),
            pltpu.VMEM((rank, comps, rz, rx, ry), F32),
            pltpu.VMEM((cz, rz, comps, rx, ry), F32),
            pltpu.VMEM((cz, rz, comps, rx, ry), F32),
            pltpu.VMEM((2, jz * nx, ry), F32),
            pltpu.VMEM((SUBSTEPS, 2, packed, ny), F32),
            pltpu.VMEM((SUBSTEPS, 2, packed, ny), F32),
            pltpu.VMEM((SUBSTEPS, 2, nx, LANES), F32),
            pltpu.VMEM((SUBSTEPS, 2, nx, LANES), F32),
            pltpu.VMEM((SUBSTEPS, 2, comps + 1, nx, ny), BF16),
            pltpu.VMEM((SUBSTEPS, 2, comps + 1, nx, ny), BF16),
            dma((cx * cy - 1,)),
            dma((cx * cy - 1,)),
            dma((cz,)),
            dma((cz,)),
            dma((SUBSTEPS, 3, 2)),
            dma((SUBSTEPS, 3, 2)),
            dma((rz, 2)),
        ],
        compiler_params=pltpu.CompilerParams(
            collective_id=0, has_side_effects=True, vmem_limit_bytes=56 * 1024 * 1024
        ),
    )(magnet, grains, stiff_tab, sat_tab, kx, ky, kz, jnp.transpose(mix, (1, 2, 0)))


def solution(mesh):
    dims = tuple(mesh.shape[name] for name in ("gx", "gy", "gz"))
    in_specs = (P(None, "gz", "gx", "gy"), P("gz", "gx", "gy"), P(), P(), P(), P(), P(), P())
    out_specs = (P(None, "gz", "gx", "gy"), P("gz", None, "gx", "gy"))
    return jax.shard_map(
        functools.partial(local, dims), mesh=mesh, in_specs=in_specs, out_specs=out_specs,
        check_vma=False,
    )
```

```python
import functools

import jax
import jax.numpy as jnp
from jax import lax
from jax.experimental import pallas as pl
from jax.experimental.pallas import tpu as pltpu
from jax.sharding import PartitionSpec as P

SUBSTEPS = 3
TIME_STEP = 0.02
DAMPING = 0.3
LANES = 128
HIGHEST = lax.Precision.HIGHEST
MESH = pl.DeviceIdType.MESH
F32 = jnp.float32
BF16 = jnp.bfloat16


def precess(m, h):
    comps = len(m)
    t = [
        m[1] * h[2] - m[2] * h[1],
        m[2] * h[0] - m[0] * h[2],
        m[0] * h[1] - m[1] * h[0],
    ]
    u = [
        m[1] * t[2] - m[2] * t[1],
        m[2] * t[0] - m[0] * t[2],
        m[0] * t[1] - m[1] * t[0],
    ]
    raw = [m[j] - TIME_STEP * (t[j] + DAMPING * u[j]) for j in range(comps)]
    shrink = lax.rsqrt(raw[0] * raw[0] + raw[1] * raw[1] + raw[2] * raw[2])
    return [part * shrink for part in raw]


def finish(m, h, demag, out_m, out_d, held, sems):
    comps, nz = m.shape[:2]
    copies = [pltpu.make_async_copy(demag, out_d, sems.at[nz])]
    copies[0].start()
    for z in range(nz):
        new = precess([m[j, z] for j in range(comps)], [h[j, z] for j in range(comps)])
        for j in range(comps):
            held[j, z] = new[j]
        copies.append(pltpu.make_async_copy(held.at[:, z], out_m.at[:, z], sems.at[z]))
        copies[-1].start()
    for copy in copies:
        copy.wait()


def kernel(
    dims,
    magnet_in, grains_in, stiff_tab, sat_tab, kx, ky, kz, mix,
    out_m, out_h, out_d,
    state, grains, stiff, inv_sat, weights, weight_x, weight_y, field_in, pooled_in, pooled, gathered, kx32, ky32, kz32, flat_x,
    mat_x, mat_y, trans_x, mixed, z_send, z_recv, fine,
    xs, xr, ys, yr, zs, zr,
    g_send, g_recv, s_send, s_recv, h_send, h_recv, in_sem,
):
    cx, cy, cz = dims
    comps, nz, nx, ny = magnet_in.shape
    rank = kx.shape[0]
    mats = stiff_tab.shape[0]
    rz, rx, ry = nz // 2, nx // 2, ny // 2
    gx_all, gy_all, gz_all = rx * cx, ry * cy, rz * cz
    jz = comps * rz
    ix, iy, iz = lax.axis_index("gx"), lax.axis_index("gy"), lax.axis_index("gz")
    plane = cx * cy
    me = ix * cy + iy

    def spot(number):
        return lax.div(number, cy), lax.rem(number, cy)

    def load(zc):
        pair = pl.ds(2 * zc, 2)
        return (
            pltpu.make_async_copy(grains_in.at[pair], grains.at[pair], in_sem.at[zc, 0]),
            pltpu.make_async_copy(
                magnet_in.at[:, pair], state.at[0, :, pair], in_sem.at[zc, 1]
            ),
        )

    for zc in range(rz):
        for copy in load(zc):
            copy.start()

    barrier = pltpu.get_barrier_semaphore()
    for d in range(1, plane):
        tx, ty = spot(lax.rem(me + d, plane))
        pl.semaphore_signal(
            barrier, inc=1, device_id={"gx": tx, "gy": ty, "gz": iz}, device_id_type=MESH
        )
    for d in range(1, cz):
        pl.semaphore_signal(
            barrier, inc=1,
            device_id={"gx": ix, "gy": iy, "gz": lax.rem(iz + d, cz)}, device_id_type=MESH,
        )

    row = lax.broadcasted_iota(jnp.int32, (nx, ny), 0)
    lane = lax.broadcasted_iota(jnp.int32, (nx, ny), 1)
    pack_lane = lax.broadcasted_iota(jnp.int32, (nx, LANES), 1)

    kx32[...] = kx[...].astype(F32)
    ky32[...] = ky[...].astype(F32)
    kz32[...] = jnp.zeros_like(kz32)
    kz32[:, 0:kz.shape[1]] = kz[...].astype(F32)

    def skewed(line, width):
        rows = jnp.broadcast_to(line, (8, width))
        place = lax.broadcasted_iota(jnp.int32, (8, width), 0)
        for step in (1, 2, 4):
            rows = jnp.where(place & step != 0, pltpu.roll(rows, step, 1), rows)
        return rows

    wide = 2 * gx_all
    lane_x = lax.broadcasted_iota(jnp.int32, (8, wide), 1)
    kx_here = pltpu.roll(kx32[...], lax.rem(2 * wide - gx_all - ix * rx, wide), 1)
    bases = [skewed(kx_here[r:r + 1, :], wide) for r in range(rank)]
    for t in range(gx_all // 8):
        block = jnp.zeros((8, wide), F32)
        for r in range(rank):
            turned = pltpu.roll(bases[r], (8 * t + r * rx) % wide, 1)
            block = jnp.where(lane_x // rx == r, turned, block)
        flat_x[8 * t:8 * t + 8, :] = block[:, 0:rank * rx]
    mat_x[...] = jnp.transpose(flat_x[...]).astype(BF16)
    def lookup(g, table):
        value = jnp.full((nx, ny), table[0], F32)
        for k in range(1, mats):
            value = jnp.where(g == k, table[k], value)
        return value

    for zc in range(rz):
        for copy in load(zc):
            copy.wait()
        sums = [None] * comps
        for half in range(2):
            z = 2 * zc + half
            s = lookup(grains[z], sat_tab)
            inv_sat[z] = 2.0 / s
            for j in range(comps):
                m = state[0, j, z]
                sums[j] = s * m if half == 0 else sums[j] + s * m
        for j in range(comps):
            pooled_in[(j * rz + zc) * nx:(j * rz + zc + 1) * nx, :] = sums[j]
    fold = (
        lax.broadcasted_iota(jnp.int32, (ny, ry), 0) // 2
        == lax.broadcasted_iota(jnp.int32, (ny, ry), 1)
    ).astype(F32)
    pooled[...] = jnp.dot(
        pooled_in[...], fold, precision=HIGHEST, preferred_element_type=F32
    )
    coarse = 0.125 * (
        pooled[pl.ds(0, jz * rx, 2), :] + pooled[pl.ds(1, jz * rx, 2), :]
    )

    def block_of(px, py):
        return gathered.at[
            :, pl.ds(pl.multiple_of(px * rx, rx), rx), pl.ds(pl.multiple_of(py * ry, ry), ry)
        ]

    block_of(ix, iy)[...] = coarse.astype(BF16).reshape(jz, rx, ry)

    pl.semaphore_wait(barrier, plane - 1 + cz - 1)

    def gather_copy(d, source):
        px, py = spot(source)
        tx, ty = spot(lax.rem(me + d, plane))
        return pltpu.make_async_remote_copy(
            src_ref=block_of(px, py), dst_ref=block_of(px, py),
            send_sem=g_send.at[d - 1], recv_sem=g_recv.at[d - 1],
            device_id={"gx": tx, "gy": ty, "gz": iz}, device_id_type=MESH,
        )

    for d in range(1, plane):
        gather_copy(d, me).start()

    def pack(step, k, value, edges):
        xs[step, 0, k:k + 1, :] = value[0:1, :]
        xs[step, 1, k:k + 1, :] = value[nx - 1:nx, :]
        hit = pack_lane == k
        return (
            jnp.where(hit, value[:, 0:1], edges[0]),
            jnp.where(hit, value[:, ny - 1:ny], edges[1]),
        )

    for z in range(nz):
        stiff[z] = lookup(grains[z], stiff_tab)
    edges = (jnp.zeros((nx, LANES), F32),) * 2
    for j in range(comps + 1):
        for z in range(nz):
            value = state[0, j, z] if j < comps else stiff[z]
            edges = pack(0, j * nz + z, value, edges)
            if z == 0:
                zs[0, 0, j] = value.astype(BF16)
            if z == nz - 1:
                zs[0, 1, j] = value.astype(BF16)
    ys[0, 0], ys[0, 1] = edges

    places = (ix, iy, iz)
    counts = (cx, cy, cz)
    names = ("gx", "gy", "gz")

    def halo_copy(step, axis, way):
        sends, recvs = ((xs, xr), (ys, yr), (zs, zr))[axis]
        src, dst = sends.at[step, way], recvs.at[step, 1 - way]
        if axis == 2 and step > 0:
            src, dst = src.at[0:comps], dst.at[0:comps]
        target = dict(zip(names, places))
        target[names[axis]] = places[axis] + (2 * way - 1)
        return pltpu.make_async_remote_copy(
            src_ref=src, dst_ref=dst,
            send_sem=h_send.at[step, axis, way], recv_sem=h_recv.at[step, axis, way],
            device_id=target, device_id_type=MESH,
        )

    def can_send(axis, way):
        return places[axis] > 0 if way == 0 else places[axis] < counts[axis] - 1

    def send_halos(step, axes, ways=(0, 1)):
        for axis in axes:
            for way in ways:
                @pl.when(can_send(axis, way))
                def _():
                    halo_copy(step, axis, way).start()

    def receive_halos(step):
        for axis in range(3):
            for way in range(2):
                @pl.when(can_send(axis, 1 - way))
                def _():
                    halo_copy(step, axis, way).wait_recv()

    send_halos(0, (2, 1, 0))

    for axis in range(3):
        recvs = (xr, yr, zr)[axis]
        for way in range(2):
            @pl.when(jnp.logical_not(can_send(axis, way)))
            def _():
                for step in range(SUBSTEPS):
                    recvs[step, way] = jnp.zeros(recvs.shape[2:], recvs.dtype)

    for c in range(cy):
        start = pl.multiple_of(ry * (iy - c) + gy_all - ry, ry)
        window = ky32[:, pl.ds(start, 2 * ry)]
        for r in range(rank):
            base = skewed(window[r:r + 1, :], 2 * ry)
            for t in range(0, ry // 8, 2):
                pair = jnp.concatenate(
                    [pltpu.roll(base, 8 * (t + e) + ry, 1)[:, 0:ry] for e in range(2)], axis=0
                )
                mat_y[r, c * ry + 8 * t:c * ry + 8 * t + 16, :] = pair.astype(BF16)

    for d in range(1, plane):
        gather_copy(d, lax.rem(me + plane - d, plane)).wait_recv()

    for t in range(jz):
        along = jnp.dot(mat_x[...], gathered[t], preferred_element_type=F32).astype(BF16)
        trans_x[:, t * rx:(t + 1) * rx, :] = along.reshape(rank, rx, gy_all)
    for r in range(rank):
        along = jnp.dot(trans_x[r], mat_y[r], preferred_element_type=F32)
        along = along.astype(BF16).astype(F32).reshape(comps, rz, rx, ry)
        for i in range(comps):
            total = mix[i, 0, r] * along[0]
            for j in range(1, comps):
                total = total + mix[i, j, r] * along[j]
            mixed[r, i] = total
    def sum_copy(peer, slot):
        return pltpu.make_async_remote_copy(
            src_ref=z_send.at[peer], dst_ref=z_recv.at[slot],
            send_sem=s_send.at[peer], recv_sem=s_recv.at[slot],
            device_id={"gx": ix, "gy": iy, "gz": peer}, device_id_type=MESH,
        )

    for n in range(cz):
        d = (cz // 2 + n) % cz if n < cz - cz // 2 else cz - n - 1
        p = lax.rem(iz + d, cz) if d else iz
        turn = lax.rem(2 * LANES + rz - 1 + rz * (iz - p) - gz_all, LANES)
        turned_z = pltpu.roll(kz32[...], turn, 1)
        totals = [[jnp.zeros((rx, ry), F32) for _ in range(comps)] for _ in range(rz)]
        for r in range(rank):
            for al in range(rz):
                for zl in range(rz):
                    at = al - zl + rz - 1
                    factor = turned_z[r:r + 1, at:at + 1]
                    for i in range(comps):
                        totals[al][i] = totals[al][i] + factor * mixed[r, i, zl]
        target = z_send if d else z_recv
        for al in range(rz):
            for i in range(comps):
                target[p, al, i] = totals[al][i]
        if d:
            sum_copy(p, iz).start()

    receive_halos(0)

    def rolled(value):
        return (
            pltpu.roll(value, 1, 0), pltpu.roll(value, nx - 1, 0),
            pltpu.roll(value, 1, 1), pltpu.roll(value, ny - 1, 1),
        )

    row_top = lax.broadcasted_iota(jnp.int32, (8, ny), 0)
    for z in range(nz):
        here = stiff[z]
        k = comps * nz + z
        below = zr[0, 0, comps].astype(F32) if z == 0 else stiff[z - 1]
        above = zr[0, 1, comps].astype(F32) if z == nz - 1 else stiff[z + 1]
        scale = 2.0 * inv_sat[z] * here
        outside = (row == 0, row == nx - 1, lane == 0, lane == ny - 1)
        for n, near in enumerate(rolled(here)):
            weights[n, z] = jnp.where(outside[n], 0.0, scale * near / (here + near))
        weights[4, z] = scale * below / (here + below)
        weights[5, z] = scale * above / (here + above)
        for way in range(2):
            cut = slice(0, 8) if way == 0 else slice(nx - 8, nx)
            near = xr[0, way, k:k + 1, :]
            weight_x[way, z] = jnp.where(
                row_top == 7 * way, scale[cut] * near / (here[cut] + near), 0.0
            )
            cut = slice(0, LANES) if way == 0 else slice(ny - LANES, ny)
            near = yr[0, way][:, k:k + 1]
            weight_y[way, z] = jnp.where(
                pack_lane == (LANES - 1) * way,
                scale[:, cut] * near / (here[:, cut] + near), 0.0,
            )

    def inner_field(now, z, j):
        near = rolled(state[now, j, z])
        field = weights[0, z] * near[0]
        for n in range(1, 4):
            field = field + weights[n, z] * near[n]
        if z > 0:
            field = field + weights[4, z] * state[now, j, z - 1]
        if z < nz - 1:
            field = field + weights[5, z] * state[now, j, z + 1]
        return field

    def outer_field(field, step, z, j):
        k = j * nz + z
        if z == 0:
            field = field + weights[4, z] * zr[step, 0, j].astype(F32)
        if z == nz - 1:
            field = field + weights[5, z] * zr[step, 1, j].astype(F32)
        top = field[0:8] + weight_x[0, z] * xr[step, 0, k:k + 1, :]
        bottom = field[nx - 8:nx] + weight_x[1, z] * xr[step, 1, k:k + 1, :]
        field = jnp.concatenate([top, field[8:nx - 8], bottom], axis=0)
        left = field[:, 0:LANES] + weight_y[0, z] * yr[step, 0][:, k:k + 1]
        right = field[:, ny - LANES:ny] + weight_y[1, z] * yr[step, 1][:, k:k + 1]
        middle = [field[:, LANES:ny - LANES]] if ny > 2 * LANES else []
        return jnp.concatenate([left] + middle + [right], axis=1)

    for z in range(nz):
        for j in range(comps):
            field_in[j, z] = outer_field(inner_field(0, z, j), 0, z, j)

    for p in range(cz):
        @pl.when(iz != p)
        def _():
            sum_copy(jnp.int32(p), p).wait_recv()

    total = z_recv[0]
    for p in range(1, cz):
        total = total + z_recv[p]
    out_d[...] = total
    unfold = (
        lax.broadcasted_iota(jnp.int32, (ry, ny), 1) // 2
        == lax.broadcasted_iota(jnp.int32, (ry, ny), 0)
    ).astype(F32)
    spread = jnp.dot(
        total.reshape(rz * comps * rx, ry), unfold, precision=HIGHEST,
        preferred_element_type=F32,
    )
    for part in range(2):
        piece = spread[:, part * ry:(part + 1) * ry]
        for odd in range(2):
            fine.at[part][pl.ds(odd, rz * comps * rx, 2), :] = piece

    def demag_at(z, j):
        at = ((z // 2) * comps + j) * nx
        return jnp.concatenate([fine[0, at:at + nx, :], fine[1, at:at + nx, :]], axis=1)

    for step in range(SUBSTEPS):
        now, later = step % 2, (step + 1) % 2
        last = step == SUBSTEPS - 1
        if step > 0:
            receive_halos(step)
        edges = (jnp.zeros((nx, LANES), F32),) * 2
        for z in [0, nz - 1] + list(range(1, nz - 1)):
            m, h = [], []
            for j in range(comps):
                m.append(state[now, j, z])
                field = field_in[j, z]
                if step == 0:
                    h.append(field + demag_at(z, j))
                else:
                    h.append(outer_field(field, step, z, j))
            if last:
                for j in range(comps):
                    out_m[j, z], out_h[j, z] = m[j], h[j]
                continue
            turned_m = precess(m, h)
            for j in range(comps):
                value = turned_m[j]
                state[later, j, z] = value
                edges = pack(step + 1, j * nz + z, value, edges)
                if z == 0:
                    zs[step + 1, 0, j] = value.astype(BF16)
                if z == nz - 1:
                    zs[step + 1, 1, j] = value.astype(BF16)
            if not last and z == 0:
                send_halos(step + 1, (2,), (0,))
            if not last and z == nz - 1:
                send_halos(step + 1, (2,), (1,))
        if not last:
            ys[step + 1, 0], ys[step + 1, 1] = edges
            send_halos(step + 1, (1, 0))
            for z in range(nz):
                for j in range(comps):
                    field_in[j, z] = inner_field(later, z, j) + demag_at(z, j)

    for d in range(1, plane):
        gather_copy(d, me).wait_send()
    for p in range(cz):
        @pl.when(iz != p)
        def _():
            sum_copy(jnp.int32(p), iz).wait_send()
    for step in range(SUBSTEPS):
        for axis in range(3):
            for way in range(2):
                @pl.when(can_send(axis, way))
                def _():
                    halo_copy(step, axis, way).wait_send()


def local(dims, magnet, grains, stiff_tab, sat_tab, kx, ky, kz, mix):
    cx, cy, cz = dims
    comps, nz, nx, ny = magnet.shape
    rank = kx.shape[0]
    rz, rx, ry = nz // 2, nx // 2, ny // 2
    jz = comps * rz
    gx_all, gy_all = rx * cx, ry * cy
    packed = (comps + 1) * nz
    vmem = pl.BlockSpec(memory_space=pltpu.VMEM)
    hbm = pl.BlockSpec(memory_space=pltpu.HBM)
    smem = pl.BlockSpec(memory_space=pltpu.SMEM)
    dma = pltpu.SemaphoreType.DMA
    m, h, demag = pl.pallas_call(
        functools.partial(kernel, dims),
        out_shape=(
            pltpu.VMEM(magnet.shape, F32),
            pltpu.VMEM(magnet.shape, F32),
            pltpu.VMEM((rz, comps, rx, ry), F32),
        ),
        in_specs=[hbm, hbm, smem, smem, vmem, vmem, vmem, smem],
        out_specs=(vmem, vmem, vmem),
        scratch_shapes=[
            pltpu.VMEM((2, comps, nz, nx, ny), F32),
            pltpu.VMEM((nz, nx, ny), jnp.int32),
            pltpu.VMEM((nz, nx, ny), F32),
            pltpu.VMEM((nz, nx, ny), F32),
            pltpu.VMEM((6, nz, nx, ny), F32),
            pltpu.VMEM((2, nz, 8, ny), F32),
            pltpu.VMEM((2, nz, nx, LANES), F32),
            pltpu.VMEM((comps, nz, nx, ny), F32),
            pltpu.VMEM((jz * nx, ny), F32),
            pltpu.VMEM((jz * nx, ry), F32),
            pltpu.VMEM((jz, gx_all, gy_all), BF16),
            pltpu.VMEM(kx.shape, F32),
            pltpu.VMEM(ky.shape, F32),
            pltpu.VMEM((rank, LANES), F32),
            pltpu.VMEM((gx_all, rank * rx), F32),
            pltpu.VMEM((rank * rx, gx_all), BF16),
            pltpu.VMEM((rank, gy_all, ry), BF16),
            pltpu.VMEM((rank, jz * rx, gy_all), BF16),
            pltpu.VMEM((rank, comps, rz, rx, ry), F32),
            pltpu.VMEM((cz, rz, comps, rx, ry), F32),
            pltpu.VMEM((cz, rz, comps, rx, ry), F32),
            pltpu.VMEM((2, jz * nx, ry), F32),
            pltpu.VMEM((SUBSTEPS, 2, packed, ny), F32),
            pltpu.VMEM((SUBSTEPS, 2, packed, ny), F32),
            pltpu.VMEM((SUBSTEPS, 2, nx, LANES), F32),
            pltpu.VMEM((SUBSTEPS, 2, nx, LANES), F32),
            pltpu.VMEM((SUBSTEPS, 2, comps + 1, nx, ny), BF16),
            pltpu.VMEM((SUBSTEPS, 2, comps + 1, nx, ny), BF16),
            dma((cx * cy - 1,)),
            dma((cx * cy - 1,)),
            dma((cz,)),
            dma((cz,)),
            dma((SUBSTEPS, 3, 2)),
            dma((SUBSTEPS, 3, 2)),
            dma((rz, 2)),
        ],
        compiler_params=pltpu.CompilerParams(
            collective_id=0, has_side_effects=True, vmem_limit_bytes=56 * 1024 * 1024
        ),
    )(magnet, grains, stiff_tab, sat_tab, kx, ky, kz, jnp.transpose(mix, (1, 2, 0)))
    return pl.pallas_call(
        finish,
        out_shape=(
            jax.ShapeDtypeStruct(m.shape, F32), jax.ShapeDtypeStruct(demag.shape, F32)
        ),
        in_specs=[vmem, vmem, vmem],
        out_specs=(hbm, hbm),
        scratch_shapes=[pltpu.VMEM(m.shape, F32), dma((nz + 1,))],
        compiler_params=pltpu.CompilerParams(vmem_limit_bytes=8 * 1024 * 1024),
    )(m, h, demag)


def solution(mesh):
    dims = tuple(mesh.shape[name] for name in ("gx", "gy", "gz"))
    in_specs = (P(None, "gz", "gx", "gy"), P("gz", "gx", "gy"), P(), P(), P(), P(), P(), P())
    out_specs = (P(None, "gz", "gx", "gy"), P("gz", None, "gx", "gy"))
    return jax.shard_map(
        functools.partial(local, dims), mesh=mesh, in_specs=in_specs, out_specs=out_specs,
        check_vma=False,
    )
```
